32 devices in a mesh: grp: 2 (over y), feat: 4 (over z), tgt: 2 (over x), lay: 2 (over core).
Axes of the slice: x: 2, y: 2, z: 4, core: 2. Of those that a mesh axis runs over, the one named last changes fastest.
Arguments:
- decoder: bfloat16 [2, 32768, 4608], P('lay', 'feat', 'tgt'), may hold values from -6 to 6
- value_weight: bfloat16 [2, 1024, 4608], P('lay', 'feat', 'tgt'), may hold values from -0.09375 to 0.09375
- out_weight: bfloat16 [2, 2048, 4608], P('lay', 'feat', 'tgt'), may hold values from -0.09375 to 0.09375
- target_enc: bfloat16 [2, 512, 4608], P('lay', 'grp', 'tgt'), parts along dimension 1, may hold values from -6 to 6
- target_pos: int32 [2, 512], P('lay', 'grp'), parts along dimension 1, may hold values from 0 to 31
- attention: float32 [2, 32, 32, 32], P('lay', 'grp', 'feat'), parts along dimension 1, may hold values from 0.005 to 0.05
- norm_gain: float32 [2, 3, 4608], P('lay', None, 'tgt'), may hold values from 0.1 to 1.9
- norm_rstd: float32 [2, 6, 32], P('lay', 'grp'), parts along dimension 1, may hold values from 0.5 to 2
- source_owner: int32 [8192, 1], P(('grp', 'feat')), parts along dimension 0, may hold values from 0 to 3; in each aligned block of 1024 rows (0 to 1023, 1024 to 2047, ...) at most 512 rows name the same one
- source_row: int32 [8192], P(('grp', 'feat')), parts along dimension 0, may hold values from 0 to 8191
- source_act: float32 [8192], P(('grp', 'feat')), parts along dimension 0, may hold values from 0.25 to 2
- source_valid: int32 [8192], P(('grp', 'feat')), parts along dimension 0, may hold values 0 or 1
Outputs:
- edges: bfloat16 [2, 512, 4096], P('lay', ('grp', 'tgt'), 'feat'), parts along dimension 1
The draws below stay inside these ranges and needn't reach their ends.
There are 2 independent parts, one for each index of `grp`. The reference program is written for one: setup_inputs(seed, part) draws one part's arguments, and reference() takes and returns one part's arrays. A program takes and returns all parts, laid end to end along the dimension named above; an argument that names none is the same for every part. Nothing has to cross between parts.
Inputs may be any that keep to these rules, and one draw needn't show every extreme that they name: `source_owner`: in each aligned block of 1024 slots (the source slots of one index of feat), no shard is named by more than 512 slots, a bound that some block reaches.
All inputs are finite; a program needn't handle non-finite values. No bound on the sum of `source_valid` on one device may be relied on, other than what follows from the above.
Results may differ from the reference program's by a relative error of at most 0.012.
Values may be sent and summed in bfloat16 or wider, within the bound.
A program may use at most 192 MiB of HBM per device.

```python
import math
import jax
import jax.numpy as jnp
import numpy as np
from jax import lax

D = 4608
HEADS = 16
KV = 8
HD = 128
NF = 32768
K = 128
LT = 2
TOKENS = 32
NT = 256
SRC = 4096
SRC_DEV = 1024
ROWS = 8192
CAP = 512
QC = 2048
KVC = 1024
N_FEAT = 4
N_TGT = 2


def set_ends(drawn, stream_key, least, high):
    longest = drawn.shape.index(max(drawn.shape))
    spots = []
    for shift in (0, 1):
        where = [jax.random.randint(jax.random.fold_in(stream_key, axis), (), 0, length) for axis, length in enumerate(drawn.shape)]
        where[longest] = (where[longest] + shift) % drawn.shape[longest]
        spots.append(tuple(where))
    return drawn.at[spots[0]].set(least).at[spots[1]].set(high)


def level_of(own_key, dims, cuts, low, high):
    def one(position, shards_of):
        draws = jax.random.uniform(jax.random.fold_in(jax.random.fold_in(own_key, 6), position), (shards_of,), jnp.float32, low / len(cuts), high / len(cuts))
        return jnp.repeat(jnp.exp(draws), dims[position] // shards_of).reshape((-1,) + (1,) * (len(dims) - position - 1))

    level = one(*cuts[0])
    for cut in cuts[1:]:
        level = level * one(*cut)
    return level


def shared_out(rng, own, number, rows, amount, top, reach, skew):
    sequence = jax.random.permutation(rng, amount)
    heavy_load, ordinary = shares(amount, rows * top, reach, skew, True), shares(amount, rows * top, reach, skew, False)
    places = jnp.arange(amount)

    def named(lengths, rotation):
        used = int((lengths > 0).sum())
        fixed = max(1, used // 4)
        moved = fixed + (places - fixed + rotation * (used - fixed)) % max(1, amount - fixed)
        return jnp.zeros((amount,), jnp.int32).at[sequence[jnp.where(places < fixed, places, moved)]].set(jnp.asarray(lengths, jnp.int32))

    lengths = jnp.where(number % 4 == 0, named(heavy_load, number // 4), named(ordinary, number - number // 4 - 1))
    mixed = jax.random.permutation(jax.random.fold_in(own, 3), amount)
    source_of, taker = mixed[0:amount // 2 * 2:2], mixed[1:amount // 2 * 2:2]
    margin = jnp.minimum(lengths[source_of] - 1, reach - lengths[taker]) // 2
    margin = jnp.where((source_of == sequence[0]) | (taker == sequence[0]) | (lengths[taker] == 0), 0, jnp.maximum(margin, 0))
    moved = jax.random.randint(jax.random.fold_in(own, 4), (amount // 2,), 0, 1 << 20) % (margin + 1)
    lengths = lengths.at[source_of].add(-moved).at[taker].add(moved)
    items = jnp.searchsorted(jnp.cumsum(lengths), jnp.arange(rows * top), side="right").astype(jnp.int32)
    grid = items.reshape(top, rows).T
    grid = grid[jax.random.permutation(jax.random.fold_in(own, 1), rows)]
    rotation = jax.random.randint(jax.random.fold_in(own, 2), (rows, 1), 0, top)
    return jnp.take_along_axis(grid, (jnp.arange(top)[None, :] + rotation) % top, axis=1)


def shares(number_of, total, limit, slope, full):
    loads = [(1 << 20) // math.isqrt(standing ** slope) + 1 for standing in range(1, number_of + 1)]
    largest = limit if full else min(limit, max(-(-total // number_of), total * loads[0] // sum(loads)))
    least = 1 if total - largest >= number_of - 1 else 0
    given, surplus = [largest] + [least] * (number_of - 1), total - largest - least * (number_of - 1)
    while surplus > 0:
        movable = [i for i in range(1, number_of) if given[i] < largest] or [i for i in range(1, number_of) if given[i] < limit]
        whole, remaining = sum([loads[i] for i in movable]), surplus
        for i in movable:
            more = min(limit - given[i], max(1, remaining * loads[i] // whole), surplus)
            given[i] = given[i] + more
            surplus = surplus - more
    return np.array(given)


def gaussian(own_key, extent, deviation, bound, split=(), dtype=jnp.bfloat16):
    values = deviation * jax.random.normal(own_key, extent, jnp.float32)
    if split:
        values = values * level_of(own_key, extent, split, -0.22, 0.18)
    return jnp.clip(values, -bound, bound).astype(dtype)


def setup_inputs(seed: int = 0, part: int = 0) -> dict:
    splits = jax.random.split(jax.random.key(seed), 13)
    own_keys = jax.random.split(jax.random.fold_in(splits[12], part), 13)
    decoder = gaussian(splits[0], (LT, NF, D), 1.0, 6.0, ((0, 2), (1, 4), (2, 2)))
    value_weight = gaussian(splits[1], (LT, KVC, D), D ** -0.5, 0.09375, ((0, 2), (1, 4), (2, 2)))
    out_weight = gaussian(splits[2], (LT, QC, D), D ** -0.5, 0.09375, ((0, 2), (1, 4), (2, 2)))
    target_enc = gaussian(own_keys[3], (LT, NT, D), 1.0, 6.0, ((0, 2), (2, 2)))
    target_pos = set_ends(jax.random.randint(own_keys[4], (LT, NT), 0, TOKENS), jax.random.fold_in(own_keys[4], 1), 0, TOKENS - 1).astype(jnp.int32)
    attention = jnp.clip(jnp.exp(math.log(0.05) - 2.3025851 * jax.random.uniform(own_keys[5], (LT, HEADS, TOKENS, TOKENS), jnp.float32) ** level_of(own_keys[5], (LT, HEADS, TOKENS, TOKENS), ((0, 2), (2, 4)), -0.2, 0.2)), 0.005, 0.05)
    norm_gain = jnp.clip(1.0 + 0.18 * jax.random.normal(splits[6], (LT, 3, D), jnp.float32), 0.1, 1.9)
    norm_rstd = jnp.clip(jnp.exp(math.log(2.0) - 1.3862944 * jax.random.uniform(own_keys[7], (LT, 3, TOKENS), jnp.float32) ** level_of(own_keys[7], (LT, 3, TOKENS), ((0, 2),), -0.2, 0.2)), 0.5, 2.0)
    source_owner_keys = jax.random.split(jax.random.fold_in(own_keys[8], 1), SRC // SRC_DEV)
    source_owner_turns = jax.random.permutation(jax.random.fold_in(own_keys[8], 3), SRC // SRC_DEV)
    source_owner = jax.vmap(lambda own, number: shared_out(jax.random.fold_in(own_keys[8], 2), own, number, SRC_DEV, N_FEAT, 1, CAP, 2))(source_owner_keys, source_owner_turns).reshape((SRC, 1))
    source_row = set_ends(jax.random.randint(own_keys[9], (SRC,), 0, ROWS), jax.random.fold_in(own_keys[9], 1), 0, ROWS - 1).astype(jnp.int32)
    source_act = jnp.clip(jnp.exp(math.log(2.0) - 2.0794415 * jax.random.uniform(own_keys[10], (SRC,), jnp.float32) ** level_of(own_keys[10], (SRC,), ((0, 4),), -0.2, 0.2)), 0.25, 2.0)
    source_valid = set_ends((jax.random.randint(own_keys[11], (SRC,), 0, 4) < 3).astype(jnp.int32), jax.random.fold_in(own_keys[11], 1), 0, 1)
    return {"decoder": decoder, "value_weight": value_weight, "out_weight": out_weight, "target_enc": target_enc, "target_pos": target_pos, "attention": attention, "norm_gain": norm_gain, "norm_rstd": norm_rstd, "source_owner": source_owner, "source_row": source_row, "source_act": source_act, "source_valid": source_valid}


def reference(decoder, value_weight, out_weight, target_enc, target_pos, attention, norm_gain, norm_rstd, source_owner, source_row, source_act, source_valid):
    feature_ids = (source_owner[:, 0] * (NF // N_FEAT) + source_row).astype(jnp.int32)
    source_token = (jnp.arange(SRC) // K).astype(jnp.int32)
    block_width = D // N_TGT
    group = HEADS // KV
    results = []
    for layer in range(LT):
        gains = norm_gain[layer]
        positions = target_pos[layer]
        enc_scaled = (target_enc[layer].astype(jnp.float32) * gains[0] * gains[1]).astype(jnp.bfloat16)
        target_scale = norm_rstd[layer, 0][positions] * norm_rstd[layer, 1][positions]
        heads_back = jnp.dot(enc_scaled, out_weight[layer].T, preferred_element_type=jnp.float32)
        heads_back = (heads_back * target_scale[:, None]).astype(jnp.bfloat16)
        head_groups = heads_back.astype(jnp.float32).reshape(NT, KV, group, HD)
        gained_values = (value_weight[layer].astype(jnp.float32) * gains[2]).astype(jnp.bfloat16)
        picked = attention[layer][:, :, positions]
        causal = jnp.arange(TOKENS)[:, None] <= positions[None, :]
        picked = jnp.where(causal[None], picked, jnp.zeros_like(picked))
        picked = jnp.transpose(picked, (1, 0, 2)).reshape(TOKENS, KV, group, NT)
        decoder_rows = decoder[layer][feature_ids].reshape(TOKENS, K, D)

        def per_token(pair):
            rows_here, weights_here = pair
            weighted = jnp.einsum('kgf,fkgc->fkc', weights_here.astype(jnp.float32), head_groups)
            weighted = weighted.reshape(NT, KV * HD).astype(jnp.bfloat16)
            total = jnp.zeros((NT, K), jnp.float32)
            for block in range(N_TGT):
                lower = block * block_width
                projected = jnp.dot(rows_here[:, lower:lower + block_width], gained_values[:, lower:lower + block_width].T, preferred_element_type=jnp.float32).astype(jnp.bfloat16)
                total = total + jnp.dot(weighted, projected.T, preferred_element_type=jnp.float32)
            return total

        scores = lax.map(per_token, (decoder_rows, picked))
        scores = jnp.transpose(scores, (1, 0, 2)).reshape(NT, SRC)
        source_scale = norm_rstd[layer, 2][source_token] * source_act * source_valid.astype(jnp.float32)
        results.append((scores * source_scale[None, :]).astype(jnp.bfloat16))
    return jnp.stack(results)
```

```python
import functools
import jax
import jax.numpy as jnp
from jax import lax
from jax.experimental import pallas as pl
from jax.experimental.pallas import tpu as pltpu
from jax.sharding import PartitionSpec as P

HEADS = 16
KV = 8
HD = 128
K = 128


def score_kernel(rows_ref, values_ref, heads_ref, picked_ref, token_ref, out_ref):
    group = HEADS // KV
    projected = lax.dot_general(
        values_ref[...],
        rows_ref[...],
        (((1,), (1,)), ((), ())),
        preferred_element_type=jnp.float32,
    ).astype(jnp.bfloat16)
    tokens = picked_ref.shape[2]
    slots = token_ref.shape[1]
    which = lax.broadcasted_iota(jnp.int32, (tokens, slots), 0) == token_ref[...]
    which = jnp.where(which, 1.0, 0.0).astype(jnp.bfloat16)
    total = jnp.zeros(out_ref.shape, jnp.float32)
    for head in range(HEADS):
        kv = head // group
        match = jnp.dot(
            heads_ref[:, head * HD : (head + 1) * HD],
            projected[kv * HD : (kv + 1) * HD],
            preferred_element_type=jnp.float32,
        )
        weight = jnp.dot(picked_ref[head], which, preferred_element_type=jnp.float32)
        total = total + match * weight
    out_ref[...] = total.astype(jnp.bfloat16)


def owner_scores(rows, values, heads, picked, tokens_of_slot):
    slots, width = rows.shape
    targets = heads.shape[0]
    block = 256
    return pl.pallas_call(
        score_kernel,
        grid=(slots // block,),
        in_specs=[
            pl.BlockSpec((block, width), lambda i: (i, 0)),
            pl.BlockSpec(values.shape, lambda i: (0, 0)),
            pl.BlockSpec(heads.shape, lambda i: (0, 0)),
            pl.BlockSpec(picked.shape, lambda i: (0, 0, 0)),
            pl.BlockSpec((1, block), lambda i: (0, i)),
        ],
        out_specs=pl.BlockSpec((targets, block), lambda i: (0, i)),
        out_shape=jax.ShapeDtypeStruct((targets, slots), jnp.bfloat16),
        compiler_params=pltpu.CompilerParams(vmem_limit_bytes=48 * 1024 * 1024),
    )(rows, values, heads, picked, tokens_of_slot)


def place_kernel(replies_ref, place_ref, scale_ref, out_ref):
    capacity = replies_ref.shape[2]
    slots = place_ref.shape[1]
    total = jnp.zeros(out_ref.shape, jnp.float32)
    spots = lax.broadcasted_iota(jnp.int32, (capacity, slots), 0)
    for owner in range(replies_ref.shape[0]):
        which = jnp.where(spots + owner * capacity == place_ref[...], 1.0, 0.0)
        total = total + jnp.dot(
            replies_ref[owner], which.astype(jnp.bfloat16), preferred_element_type=jnp.float32
        )
    out_ref[...] = (total * scale_ref[...]).astype(jnp.bfloat16)


def on_device(
    decoder,
    value_weight,
    out_weight,
    target_enc,
    target_pos,
    attention,
    norm_gain,
    norm_rstd,
    source_owner,
    source_row,
    source_act,
    source_valid,
):
    n_feat = lax.axis_size("feat")
    n_tgt = lax.axis_size("tgt")
    me_tgt = lax.axis_index("tgt")
    shard = decoder[0]
    shard_rows = shard.shape[0]
    slot_count = source_row.shape[0]
    capacity = max(2, 2 * slot_count // n_feat)
    gains = norm_gain[0]
    positions = target_pos[0]
    targets = positions.shape[0]
    owners = source_owner[:, 0]

    def shifted(x, step):
        return lax.ppermute(x, "tgt", [(i, (i + step) % n_tgt) for i in range(n_tgt)])

    gained_values = (value_weight[0].astype(jnp.float32) * gains[2]).astype(jnp.bfloat16)
    values = lax.all_gather(gained_values, "feat", axis=0, tiled=True)

    member = (owners[:, None] == jnp.arange(n_feat, dtype=jnp.int32)[None, :]).astype(jnp.int32)
    ranks = jnp.sum((jnp.cumsum(member, axis=0) - 1) * member, axis=1)
    flat_slot = owners * capacity + ranks
    token_here = jnp.arange(slot_count, dtype=jnp.int32) // K
    asked = jnp.sum(
        jnp.where(
            flat_slot[None, :] == jnp.arange(n_feat * capacity, dtype=jnp.int32)[:, None],
            (token_here * shard_rows + source_row)[None, :],
            0,
        ),
        axis=1,
    )
    asked = lax.all_to_all(
        asked.reshape(n_feat, capacity), "feat", split_axis=0, concat_axis=0, tiled=True
    )
    rows = shard.at[(asked % shard_rows).reshape(-1)].get(mode="promise_in_bounds")
    tok_dev = attention.shape[2]
    tokens_of_slot = asked // shard_rows + (
        jnp.arange(n_feat, dtype=jnp.int32) * tok_dev
    )[:, None]

    rstd_table = norm_rstd[0]
    tokens_all = rstd_table.shape[1]
    pos_table = (positions[:, None] == jnp.arange(tokens_all, dtype=jnp.int32)[None, :]).astype(
        jnp.float32
    )
    target_scale = jnp.dot(
        pos_table, rstd_table[0] * rstd_table[1], precision=lax.Precision.HIGHEST
    )
    enc_scaled = (target_enc[0].astype(jnp.float32) * gains[0] * gains[1]).astype(jnp.bfloat16)
    partial_heads = jnp.dot(enc_scaled, out_weight[0].T, preferred_element_type=jnp.float32)
    summed_heads = partial_heads
    for step in range(1, n_tgt):
        summed_heads = summed_heads + shifted(partial_heads, step)
    heads_local = (summed_heads * target_scale[:, None]).astype(jnp.bfloat16)
    heads_back = lax.all_gather(heads_local, "feat", axis=1, tiled=True)

    attn_all = lax.all_gather(attention[0].astype(jnp.bfloat16), "feat", axis=1, tiled=True)
    chosen = jnp.einsum(
        "fq,htq->hft",
        pos_table.astype(jnp.bfloat16),
        attn_all,
        preferred_element_type=jnp.float32,
    )
    causal = jnp.arange(tokens_all, dtype=jnp.int32)[None, :] <= positions[:, None]
    picked = jnp.where(causal[None], chosen, 0.0).astype(jnp.bfloat16)

    raw = owner_scores(rows, values, heads_back, picked, tokens_of_slot.reshape(1, -1))
    own_targets = targets // n_tgt

    def part(of):
        return lax.dynamic_slice_in_dim(raw, of * own_targets, own_targets)

    scores = part(me_tgt).astype(jnp.float32)
    for step in range(1, n_tgt):
        scores = scores + shifted(part((me_tgt + step) % n_tgt), step).astype(jnp.float32)
    replies = lax.all_to_all(
        scores.astype(jnp.bfloat16).reshape(own_targets, n_feat, capacity).transpose(1, 0, 2),
        "feat",
        split_axis=0,
        concat_axis=0,
        tiled=True,
    )
    local_rstd = lax.dynamic_slice_in_dim(
        rstd_table[2], lax.axis_index("feat") * tok_dev, tok_dev
    )
    source_scale = jnp.repeat(local_rstd, K) * source_act * source_valid.astype(jnp.float32)
    return pl.pallas_call(
        place_kernel,
        out_shape=jax.ShapeDtypeStruct((own_targets, slot_count), jnp.bfloat16),
        compiler_params=pltpu.CompilerParams(vmem_limit_bytes=32 * 1024 * 1024),
    )(replies, flat_slot[None, :], source_scale[None, :])[None]


def solution(mesh):
    in_specs = (
        P("lay", "feat", "tgt"),
        P("lay", "feat", "tgt"),
        P("lay", "feat", "tgt"),
        P("lay", "grp", "tgt"),
        P("lay", "grp"),
        P("lay", "grp", "feat", None),
        P("lay", None, "tgt"),
        P("lay", "grp", None),
        P(("grp", "feat"), None),
        P(("grp", "feat")),
        P(("grp", "feat")),
        P(("grp", "feat")),
    )
    out_specs = P("lay", ("grp", "tgt"), "feat")
    return jax.shard_map(
        on_device, mesh=mesh, in_specs=in_specs, out_specs=out_specs, check_vma=False
    )
```

```python
import functools
import jax
import jax.numpy as jnp
from jax import lax
from jax.experimental import pallas as pl
from jax.experimental.pallas import tpu as pltpu
from jax.sharding import PartitionSpec as P

HEADS = 16
KV = 8
HD = 128
K = 128


def gather_kernel(index_ref, shard_ref, out_ref, held, sems):
    step = pl.program_id(0)
    steps = pl.num_programs(0)
    block = out_ref.shape[0]
    width = out_ref.shape[1]

    def fetch(of, slot):
        @pl.loop(0, block, unroll=8)
        def _(i):
            pltpu.make_async_copy(
                shard_ref.at[index_ref[of * block + i] // 8], held.at[slot, i], sems.at[slot]
            ).start()

    @pl.when(step == 0)
    def _():
        fetch(0, 0)

    @pl.when(step + 1 < steps)
    def _():
        fetch(step + 1, (step + 1) % 2)

    now = step % 2
    pltpu.make_async_copy(shard_ref.at[pl.ds(0, block)], held.at[now], sems.at[now]).wait()
    sublane = lax.broadcasted_iota(jnp.int32, (8, width), 0)

    @pl.loop(0, block // 16)
    def _(chunk):
        halves = []
        for half in range(2):
            kept = jnp.zeros((8, width), jnp.float32)
            for u in range(8):
                i = chunk * 16 + half * 8 + u
                row = index_ref[step * block + i] % 8
                group = held[now, i].astype(jnp.float32)
                turned = pltpu.roll(group, (u + 8 - row) % 8, 0)
                kept = jnp.where(sublane == u, turned, kept)
            halves.append(kept)
        out_ref[pl.ds(pl.multiple_of(chunk * 16, 16), 16), :] = jnp.concatenate(
            halves, axis=0
        ).astype(jnp.bfloat16)


def gather_rows(shard, index):
    slots = index.shape[0]
    width = shard.shape[1]
    block = 64
    return pl.pallas_call(
        gather_kernel,
        grid_spec=pltpu.PrefetchScalarGridSpec(
            num_scalar_prefetch=1,
            grid=(slots // block,),
            in_specs=[pl.BlockSpec(memory_space=pl.ANY)],
            out_specs=pl.BlockSpec((block, width), lambda i, index: (i, 0)),
            scratch_shapes=[
                pltpu.VMEM((2, block, 8, width), jnp.bfloat16),
                pltpu.SemaphoreType.DMA((2,)),
            ],
        ),
        out_shape=jax.ShapeDtypeStruct((slots, width), jnp.bfloat16),
        compiler_params=pltpu.CompilerParams(vmem_limit_bytes=24 * 1024 * 1024),
        cost_estimate=pl.CostEstimate(
            flops=slots * width * 16, bytes_accessed=slots * width * 18, transcendentals=0
        ),
    )(index, shard.reshape(shard.shape[0] // 8, 8, width))


def score_kernel(kv_ref, rows_ref, values_ref, heads_ref, picked_ref, token_ref, out_ref):
    group = HEADS // KV
    projected = lax.dot_general(
        values_ref[...],
        rows_ref[...],
        (((1,), (1,)), ((), ())),
        preferred_element_type=jnp.float32,
    ).astype(jnp.bfloat16)
    tokens = picked_ref.shape[2]
    slots = token_ref.shape[1]
    which = lax.broadcasted_iota(jnp.int32, (tokens, slots), 0) == token_ref[...]
    which = jnp.where(which, 1.0, 0.0).astype(jnp.bfloat16)
    total = jnp.zeros(out_ref.shape, jnp.float32)
    for block in range(KV):
        kv = kv_ref[block]
        for g in range(group):
            match = jnp.dot(
                heads_ref[kv, :, g * HD : (g + 1) * HD],
                projected[block * HD : (block + 1) * HD],
                preferred_element_type=jnp.float32,
            )
            weight = jnp.dot(
                picked_ref[kv * group + g], which, preferred_element_type=jnp.float32
            )
            total = total + match * weight
    out_ref[...] = total.astype(jnp.bfloat16)


def owner_scores(kv_of_block, rows, values, heads, picked, tokens_of_slot):
    slots, width = rows.shape
    targets = heads.shape[1]
    block = 512
    return pl.pallas_call(
        score_kernel,
        grid=(slots // block,),
        in_specs=[
            pl.BlockSpec(memory_space=pltpu.SMEM),
            pl.BlockSpec((block, width), lambda i: (i, 0)),
            pl.BlockSpec(values.shape, lambda i: (0, 0)),
            pl.BlockSpec(heads.shape, lambda i: (0, 0, 0)),
            pl.BlockSpec(picked.shape, lambda i: (0, 0, 0)),
            pl.BlockSpec((1, block), lambda i: (0, i)),
        ],
        out_specs=pl.BlockSpec((targets, block), lambda i: (0, i)),
        out_shape=jax.ShapeDtypeStruct((targets, slots), jnp.bfloat16),
        compiler_params=pltpu.CompilerParams(vmem_limit_bytes=48 * 1024 * 1024),
    )(kv_of_block, rows, values, heads, picked, tokens_of_slot)


def place_kernel(replies_ref, place_ref, scale_ref, out_ref):
    capacity = replies_ref.shape[2]
    slots = place_ref.shape[1]
    total = jnp.zeros(out_ref.shape, jnp.float32)
    spots = lax.broadcasted_iota(jnp.int32, (capacity, slots), 0)
    for owner in range(replies_ref.shape[0]):
        which = jnp.where(spots + owner * capacity == place_ref[...], 1.0, 0.0)
        total = total + jnp.dot(
            replies_ref[owner], which.astype(jnp.bfloat16), preferred_element_type=jnp.float32
        )
    out_ref[...] = (total * scale_ref[...]).astype(jnp.bfloat16)


def on_device(
    decoder,
    value_weight,
    out_weight,
    target_enc,
    target_pos,
    attention,
    norm_gain,
    norm_rstd,
    source_owner,
    source_row,
    source_act,
    source_valid,
):
    n_feat = lax.axis_size("feat")
    n_tgt = lax.axis_size("tgt")
    me_tgt = lax.axis_index("tgt")
    shard = decoder[0]
    shard_rows = shard.shape[0]
    slot_count = source_row.shape[0]
    capacity = max(2, 2 * slot_count // n_feat)
    gains = norm_gain[0]
    positions = target_pos[0]
    targets = positions.shape[0]
    owners = source_owner[:, 0]

    def shifted(x, step):
        return lax.ppermute(x, "tgt", [(i, (i + step) % n_tgt) for i in range(n_tgt)])

    gained_values = (value_weight[0].astype(jnp.float32) * gains[2]).astype(jnp.bfloat16)
    n_grp = lax.axis_size("grp")
    me_feat = lax.axis_index("feat")
    me_grp = lax.axis_index("grp")
    whole_heads = gained_values.shape[0] == n_grp * HD and n_grp == 2
    if whole_heads:
        held = lax.dynamic_slice_in_dim(gained_values, me_grp * HD, HD)
        blocks = [gained_values]
        kv_list = [2 * me_feat, 2 * me_feat + 1]
        for step in range(1, n_feat):
            held = lax.ppermute(held, "feat", [(i, (i + 1) % n_feat) for i in range(n_feat)])
            shard_of = (me_feat - step + n_feat) % n_feat
            blocks += [held, lax.ppermute(held, "grp", [(0, 1), (1, 0)])]
            kv_list += [2 * shard_of + me_grp, 2 * shard_of + 1 - me_grp]
        values = jnp.concatenate(blocks, axis=0)
        kv_of_block = jnp.stack(kv_list).astype(jnp.int32)
    else:
        values = lax.all_gather(gained_values, "feat", axis=0, tiled=True)
        kv_of_block = jnp.arange(KV, dtype=jnp.int32)

    member = (owners[:, None] == jnp.arange(n_feat, dtype=jnp.int32)[None, :]).astype(jnp.int32)
    ranks = jnp.sum((jnp.cumsum(member, axis=0) - 1) * member, axis=1)
    flat_slot = owners * capacity + ranks
    token_here = jnp.arange(slot_count, dtype=jnp.int32) // K
    asked = jnp.sum(
        jnp.where(
            flat_slot[None, :] == jnp.arange(n_feat * capacity, dtype=jnp.int32)[:, None],
            (token_here * shard_rows + source_row)[None, :],
            0,
        ),
        axis=1,
    )
    asked = lax.all_to_all(
        asked.reshape(n_feat, capacity), "feat", split_axis=0, concat_axis=0, tiled=True
    )
    rows = gather_rows(shard, (asked % shard_rows).reshape(-1))
    tok_dev = attention.shape[2]
    tokens_of_slot = asked // shard_rows + (
        jnp.arange(n_feat, dtype=jnp.int32) * tok_dev
    )[:, None]

    rstd_table = norm_rstd[0]
    tokens_all = rstd_table.shape[1]
    pos_table = (positions[:, None] == jnp.arange(tokens_all, dtype=jnp.int32)[None, :]).astype(
        jnp.float32
    )
    target_scale = jnp.dot(
        pos_table, rstd_table[0] * rstd_table[1], precision=lax.Precision.HIGHEST
    )
    enc_scaled = (target_enc[0].astype(jnp.float32) * gains[0] * gains[1]).astype(jnp.bfloat16)
    partial_heads = jnp.dot(enc_scaled, out_weight[0].T, preferred_element_type=jnp.float32)
    summed_heads = partial_heads
    for step in range(1, n_tgt):
        summed_heads = summed_heads + shifted(partial_heads, step)
    heads_local = (summed_heads * target_scale[:, None]).astype(jnp.bfloat16)
    attn_local = attention[0].astype(jnp.bfloat16)
    pair = HEADS // KV * HD
    if whole_heads:
        own_kv = heads_local.shape[1] // pair
        sent = jnp.concatenate(
            [
                heads_local.reshape(targets, own_kv, pair).transpose(1, 0, 2).reshape(-1, pair),
                attn_local.reshape(-1, pair),
            ],
            axis=0,
        )
        got = lax.all_gather(sent, "feat", axis=0)
        heads_back = got[:, : own_kv * targets].reshape(KV, targets, pair)
        attn_all = got[:, own_kv * targets :].reshape((n_feat,) + attn_local.shape)
        attn_all = attn_all.transpose(1, 0, 2, 3).reshape(HEADS, tokens_all, tokens_all)
    else:
        heads_back = lax.all_gather(heads_local, "feat", axis=1, tiled=True)
        heads_back = heads_back.reshape(targets, KV, pair).transpose(1, 0, 2)
        attn_all = lax.all_gather(attn_local, "feat", axis=1, tiled=True)
    chosen = jnp.einsum(
        "fq,htq->hft",
        pos_table.astype(jnp.bfloat16),
        attn_all,
        preferred_element_type=jnp.float32,
    )
    causal = jnp.arange(tokens_all, dtype=jnp.int32)[None, :] <= positions[:, None]
    picked = jnp.where(causal[None], chosen, 0.0).astype(jnp.bfloat16)

    raw = owner_scores(kv_of_block, rows, values, heads_back, picked, tokens_of_slot.reshape(1, -1))
    own_targets = targets // n_tgt

    def part(of):
        return lax.dynamic_slice_in_dim(raw, of * own_targets, own_targets)

    scores = part(me_tgt).astype(jnp.float32)
    for step in range(1, n_tgt):
        scores = scores + shifted(part((me_tgt + step) % n_tgt), step).astype(jnp.float32)
    replies = lax.all_to_all(
        scores.astype(jnp.bfloat16).reshape(own_targets, n_feat, capacity).transpose(1, 0, 2),
        "feat",
        split_axis=0,
        concat_axis=0,
        tiled=True,
    )
    local_rstd = lax.dynamic_slice_in_dim(
        rstd_table[2], lax.axis_index("feat") * tok_dev, tok_dev
    )
    source_scale = jnp.repeat(local_rstd, K) * source_act * source_valid.astype(jnp.float32)
    return pl.pallas_call(
        place_kernel,
        out_shape=jax.ShapeDtypeStruct((own_targets, slot_count), jnp.bfloat16),
        compiler_params=pltpu.CompilerParams(vmem_limit_bytes=32 * 1024 * 1024),
    )(replies, flat_slot[None, :], source_scale[None, :])[None]


def solution(mesh):
    in_specs = (
        P("lay", "feat", "tgt"),
        P("lay", "feat", "tgt"),
        P("lay", "feat", "tgt"),
        P("lay", "grp", "tgt"),
        P("lay", "grp"),
        P("lay", "grp", "feat", None),
        P("lay", None, "tgt"),
        P("lay", "grp", None),
        P(("grp", "feat"), None),
        P(("grp", "feat")),
        P(("grp", "feat")),
        P(("grp", "feat")),
    )
    out_specs = P("lay", ("grp", "tgt"), "feat")
    return jax.shard_map(
        on_device, mesh=mesh, in_specs=in_specs, out_specs=out_specs, check_vma=False
    )
```

```python
import functools
import jax
import jax.numpy as jnp
from jax import lax
from jax.experimental import pallas as pl
from jax.experimental.pallas import tpu as pltpu
from jax.sharding import PartitionSpec as P

HEADS = 16
KV = 8
HD = 128
K = 128


def gather_kernel(index_ref, shard_ref, out_ref, held, sems):
    step = pl.program_id(0)
    steps = pl.num_programs(0)
    block = out_ref.shape[0]
    width = out_ref.shape[1]

    def fetch(of, slot):
        @pl.loop(0, block, unroll=8)
        def _(i):
            pltpu.make_async_copy(
                shard_ref.at[index_ref[of * block + i] // 8], held.at[slot, i], sems.at[slot]
            ).start()

    @pl.when(step == 0)
    def _():
        fetch(0, 0)

    @pl.when(step + 1 < steps)
    def _():
        fetch(step + 1, (step + 1) % 2)

    now = step % 2
    pltpu.make_async_copy(shard_ref.at[pl.ds(0, block)], held.at[now], sems.at[now]).wait()
    sublane = lax.broadcasted_iota(jnp.int32, (8, width), 0)

    @pl.loop(0, block // 16)
    def _(chunk):
        halves = []
        for half in range(2):
            kept = jnp.zeros((8, width), jnp.float32)
            for u in range(8):
                i = chunk * 16 + half * 8 + u
                row = index_ref[step * block + i] % 8
                group = held[now, i].astype(jnp.float32)
                turned = pltpu.roll(group, (u + 8 - row) % 8, 0)
                kept = jnp.where(sublane == u, turned, kept)
            halves.append(kept)
        out_ref[pl.ds(pl.multiple_of(chunk * 16, 16), 16), :] = jnp.concatenate(
            halves, axis=0
        ).astype(jnp.bfloat16)


def gather_rows(shard, index):
    slots = index.shape[0]
    width = shard.shape[1]
    block = 64
    return pl.pallas_call(
        gather_kernel,
        grid_spec=pltpu.PrefetchScalarGridSpec(
            num_scalar_prefetch=1,
            grid=(slots // block,),
            in_specs=[pl.BlockSpec(memory_space=pl.ANY)],
            out_specs=pl.BlockSpec((block, width), lambda i, index: (i, 0)),
            scratch_shapes=[
                pltpu.VMEM((2, block, 8, width), jnp.bfloat16),
                pltpu.SemaphoreType.DMA((2,)),
            ],
        ),
        out_shape=jax.ShapeDtypeStruct((slots, width), jnp.bfloat16),
        compiler_params=pltpu.CompilerParams(vmem_limit_bytes=24 * 1024 * 1024),
        cost_estimate=pl.CostEstimate(
            flops=slots * width * 16, bytes_accessed=slots * width * 18, transcendentals=0
        ),
    )(index, shard.reshape(shard.shape[0] // 8, 8, width))


def score_kernel(kv_of_block, rows_ref, values_ref, heads_ref, picked_ref, token_ref, out_ref):
    group = HEADS // KV
    projected = lax.dot_general(
        values_ref[...],
        rows_ref[...],
        (((1,), (1,)), ((), ())),
        preferred_element_type=jnp.float32,
    ).astype(jnp.bfloat16)
    tokens = picked_ref.shape[2]
    slots = token_ref.shape[1]
    which = lax.broadcasted_iota(jnp.int32, (tokens, slots), 0) == token_ref[...]
    which = jnp.where(which, 1.0, 0.0).astype(jnp.bfloat16)
    total = jnp.zeros(out_ref.shape, jnp.float32)
    for block in range(KV):
        kv = kv_of_block[block]
        for g in range(group):
            match = jnp.dot(
                heads_ref[kv, :, g * HD : (g + 1) * HD],
                projected[block * HD : (block + 1) * HD],
                preferred_element_type=jnp.float32,
            )
            weight = jnp.dot(
                picked_ref[kv * group + g], which, preferred_element_type=jnp.float32
            )
            total = total + match * weight
    out_ref[...] = total.astype(jnp.bfloat16)


def owner_scores(kv_of_block, rows, values, heads, picked, tokens_of_slot):
    slots, width = rows.shape
    targets = heads.shape[1]
    block = 512
    return pl.pallas_call(
        functools.partial(score_kernel, kv_of_block),
        grid=(slots // block,),
        in_specs=[
            pl.BlockSpec((block, width), lambda i: (i, 0)),
            pl.BlockSpec(values.shape, lambda i: (0, 0)),
            pl.BlockSpec(heads.shape, lambda i: (0, 0, 0)),
            pl.BlockSpec(picked.shape, lambda i: (0, 0, 0)),
            pl.BlockSpec((1, block), lambda i: (0, i)),
        ],
        out_specs=pl.BlockSpec((targets, block), lambda i: (0, i)),
        out_shape=jax.ShapeDtypeStruct((targets, slots), jnp.bfloat16),
        compiler_params=pltpu.CompilerParams(vmem_limit_bytes=48 * 1024 * 1024),
    )(rows, values, heads, picked, tokens_of_slot)


def place_kernel(replies_ref, place_ref, scale_ref, out_ref):
    capacity = replies_ref.shape[2]
    slots = place_ref.shape[1]
    total = jnp.zeros(out_ref.shape, jnp.float32)
    spots = lax.broadcasted_iota(jnp.int32, (capacity, slots), 0)
    for owner in range(replies_ref.shape[0]):
        which = jnp.where(spots + owner * capacity == place_ref[...], 1.0, 0.0)
        total = total + jnp.dot(
            replies_ref[owner], which.astype(jnp.bfloat16), preferred_element_type=jnp.float32
        )
    out_ref[...] = (total * scale_ref[...]).astype(jnp.bfloat16)


def on_device(
    decoder,
    value_weight,
    out_weight,
    target_enc,
    target_pos,
    attention,
    norm_gain,
    norm_rstd,
    source_owner,
    source_row,
    source_act,
    source_valid,
):
    n_feat = lax.axis_size("feat")
    n_tgt = lax.axis_size("tgt")
    me_tgt = lax.axis_index("tgt")
    shard = decoder[0]
    shard_rows = shard.shape[0]
    slot_count = source_row.shape[0]
    capacity = max(2, 2 * slot_count // n_feat)
    gains = norm_gain[0]
    positions = target_pos[0]
    targets = positions.shape[0]
    owners = source_owner[:, 0]

    def shifted(x, step):
        return lax.ppermute(x, "tgt", [(i, (i + step) % n_tgt) for i in range(n_tgt)])

    gained_values = (value_weight[0].astype(jnp.float32) * gains[2]).astype(jnp.bfloat16)
    n_grp = lax.axis_size("grp")
    me_grp = lax.axis_index("grp")
    kv_of_block = list(range(KV))
    whole_heads = gained_values.shape[0] == n_grp * HD and n_grp == 2
    if whole_heads:
        half = lax.dynamic_slice_in_dim(gained_values, me_grp * HD, HD)
        target_enc, half = lax.optimization_barrier((target_enc, half))
        kv_of_block = [n_grp * j + g for g in range(n_grp) for j in range(n_feat)]
        values = lax.all_gather(half, ("grp", "feat"), axis=0, tiled=True)
    else:
        values = lax.all_gather(gained_values, "feat", axis=0, tiled=True)

    member = (owners[:, None] == jnp.arange(n_feat, dtype=jnp.int32)[None, :]).astype(jnp.int32)
    ranks = jnp.sum((jnp.cumsum(member, axis=0) - 1) * member, axis=1)
    flat_slot = owners * capacity + ranks
    token_here = jnp.arange(slot_count, dtype=jnp.int32) // K
    asked = jnp.sum(
        jnp.where(
            flat_slot[None, :] == jnp.arange(n_feat * capacity, dtype=jnp.int32)[:, None],
            (token_here * shard_rows + source_row)[None, :],
            0,
        ),
        axis=1,
    )
    asked = lax.all_to_all(
        asked.reshape(n_feat, capacity), "feat", split_axis=0, concat_axis=0, tiled=True
    )
    rows = gather_rows(shard, (asked % shard_rows).reshape(-1))
    tok_dev = attention.shape[2]
    tokens_of_slot = asked // shard_rows + (
        jnp.arange(n_feat, dtype=jnp.int32) * tok_dev
    )[:, None]

    rstd_table = norm_rstd[0]
    tokens_all = rstd_table.shape[1]
    pos_table = (positions[:, None] == jnp.arange(tokens_all, dtype=jnp.int32)[None, :]).astype(
        jnp.float32
    )
    target_scale = jnp.dot(
        pos_table, rstd_table[0] * rstd_table[1], precision=lax.Precision.HIGHEST
    )
    enc_scaled = (target_enc[0].astype(jnp.float32) * gains[0] * gains[1]).astype(jnp.bfloat16)
    partial_heads = jnp.dot(enc_scaled, out_weight[0].T, preferred_element_type=jnp.float32)
    own_targets = targets // n_tgt

    def part(x, of):
        return lax.dynamic_slice_in_dim(x, of * own_targets, own_targets)

    summed_heads = part(partial_heads, me_tgt)
    for step in range(1, n_tgt):
        summed_heads = summed_heads + shifted(part(partial_heads, (me_tgt + step) % n_tgt), step)
    heads_local = (summed_heads * part(target_scale, me_tgt)[:, None]).astype(jnp.bfloat16)
    attn_local = attention[0].astype(jnp.bfloat16)
    pair = HEADS // KV * HD
    if whole_heads:
        own_kv = heads_local.shape[1] // pair
        attn_part = lax.dynamic_slice_in_dim(
            attn_local.reshape(n_tgt, -1, pair), me_tgt, 1
        )[0]
        sent = jnp.concatenate(
            [
                heads_local.reshape(own_targets, own_kv, pair).transpose(1, 0, 2).reshape(-1, pair),
                attn_part,
            ],
            axis=0,
        )
        got = lax.all_gather(sent, ("tgt", "feat"), axis=0)
        cut = own_kv * own_targets
        heads_back = got[:, :cut].reshape(n_tgt, n_feat, own_kv, own_targets, pair)
        heads_back = heads_back.transpose(1, 2, 0, 3, 4).reshape(KV, targets, pair)
        attn_all = got[:, cut:].reshape(n_tgt, n_feat, -1).transpose(1, 0, 2)
        attn_all = attn_all.reshape((n_feat,) + attn_local.shape)
        attn_all = attn_all.transpose(1, 0, 2, 3).reshape(HEADS, tokens_all, tokens_all)
    else:
        heads_back = lax.all_gather(heads_local, "feat", axis=1, tiled=True)
        heads_back = lax.all_gather(heads_back, "tgt", axis=0, tiled=True)
        heads_back = heads_back.reshape(targets, KV, pair).transpose(1, 0, 2)
        attn_all = lax.all_gather(attn_local, "feat", axis=1, tiled=True)
    chosen = jnp.einsum(
        "fq,htq->hft",
        pos_table.astype(jnp.bfloat16),
        attn_all,
        preferred_element_type=jnp.float32,
    )
    causal = jnp.arange(tokens_all, dtype=jnp.int32)[None, :] <= positions[:, None]
    picked = jnp.where(causal[None], chosen, 0.0).astype(jnp.bfloat16)

    raw = owner_scores(kv_of_block, rows, values, heads_back, picked, tokens_of_slot.reshape(1, -1))
    scores = part(raw, me_tgt).astype(jnp.float32)
    for step in range(1, n_tgt):
        scores = scores + shifted(part(raw, (me_tgt + step) % n_tgt), step).astype(jnp.float32)
    replies = lax.all_to_all(
        scores.astype(jnp.bfloat16).reshape(own_targets, n_feat, capacity).transpose(1, 0, 2),
        "feat",
        split_axis=0,
        concat_axis=0,
        tiled=True,
    )
    local_rstd = lax.dynamic_slice_in_dim(
        rstd_table[2], lax.axis_index("feat") * tok_dev, tok_dev
    )
    source_scale = jnp.repeat(local_rstd, K) * source_act * source_valid.astype(jnp.float32)
    return pl.pallas_call(
        place_kernel,
        out_shape=jax.ShapeDtypeStruct((own_targets, slot_count), jnp.bfloat16),
        compiler_params=pltpu.CompilerParams(vmem_limit_bytes=32 * 1024 * 1024),
    )(replies, flat_slot[None, :], source_scale[None, :])[None]


def solution(mesh):
    in_specs = (
        P("lay", "feat", "tgt"),
        P("lay", "feat", "tgt"),
        P("lay", "feat", "tgt"),
        P("lay", "grp", "tgt"),
        P("lay", "grp"),
        P("lay", "grp", "feat", None),
        P("lay", None, "tgt"),
        P("lay", "grp", None),
        P(("grp", "feat"), None),
        P(("grp", "feat")),
        P(("grp", "feat")),
        P(("grp", "feat")),
    )
    out_specs = P("lay", ("grp", "tgt"), "feat")
    return jax.shard_map(
        on_device, mesh=mesh, in_specs=in_specs, out_specs=out_specs, check_vma=False
    )
```

```python
import functools
import jax
import jax.numpy as jnp
from jax import lax
from jax.experimental import pallas as pl
from jax.experimental.pallas import tpu as pltpu
from jax.sharding import PartitionSpec as P

HEADS = 16
KV = 8
HD = 128
K = 128


def gather_kernel(index_ref, shard_ref, out_ref, held, sems):
    step = pl.program_id(0)
    steps = pl.num_programs(0)
    block = out_ref.shape[0]
    width = out_ref.shape[1]

    def fetch(of, slot):
        @pl.loop(0, block, unroll=8)
        def _(i):
            pltpu.make_async_copy(
                shard_ref.at[index_ref[of * block + i] // 8], held.at[slot, i], sems.at[slot]
            ).start()

    @pl.when(step == 0)
    def _():
        fetch(0, 0)

    @pl.when(step + 1 < steps)
    def _():
        fetch(step + 1, (step + 1) % 2)

    now = step % 2
    pltpu.make_async_copy(shard_ref.at[pl.ds(0, block)], held.at[now], sems.at[now]).wait()
    sublane = lax.broadcasted_iota(jnp.int32, (8, width), 0)

    @pl.loop(0, block // 16)
    def _(chunk):
        halves = []
        for half in range(2):
            kept = jnp.zeros((8, width), jnp.float32)
            for u in range(8):
                i = chunk * 16 + half * 8 + u
                row = index_ref[step * block + i] % 8
                group = held[now, i].astype(jnp.float32)
                turned = pltpu.roll(group, (u + 8 - row) % 8, 0)
                kept = jnp.where(sublane == u, turned, kept)
            halves.append(kept)
        out_ref[pl.ds(pl.multiple_of(chunk * 16, 16), 16), :] = jnp.concatenate(
            halves, axis=0
        ).astype(jnp.bfloat16)


def gather_rows(shard, index):
    slots = index.shape[0]
    width = shard.shape[1]
    block = 64
    return pl.pallas_call(
        gather_kernel,
        grid_spec=pltpu.PrefetchScalarGridSpec(
            num_scalar_prefetch=1,
            grid=(slots // block,),
            in_specs=[pl.BlockSpec(memory_space=pl.ANY)],
            out_specs=pl.BlockSpec((block, width), lambda i, index: (i, 0)),
            scratch_shapes=[
                pltpu.VMEM((2, block, 8, width), jnp.bfloat16),
                pltpu.SemaphoreType.DMA((2,)),
            ],
        ),
        out_shape=jax.ShapeDtypeStruct((slots, width), jnp.bfloat16),
        compiler_params=pltpu.CompilerParams(vmem_limit_bytes=24 * 1024 * 1024),
        cost_estimate=pl.CostEstimate(
            flops=slots * width * 16, bytes_accessed=slots * width * 18, transcendentals=0
        ),
    )(index, shard.reshape(shard.shape[0] // 8, 8, width))


def score_kernel(kv_of_block, rows_ref, values_ref, heads_ref, picked_ref, token_ref, out_ref):
    group = HEADS // KV
    projected = lax.dot_general(
        values_ref[...],
        rows_ref[...],
        (((1,), (1,)), ((), ())),
        preferred_element_type=jnp.float32,
    ).astype(jnp.bfloat16)
    tokens = picked_ref.shape[2]
    slots = token_ref.shape[1]
    which = lax.broadcasted_iota(jnp.int32, (tokens, slots), 0) == token_ref[...]
    which = jnp.where(which, 1.0, 0.0).astype(jnp.bfloat16)
    total = jnp.zeros(out_ref.shape, jnp.float32)
    for block in range(KV):
        kv = kv_of_block[block]
        for g in range(group):
            match = jnp.dot(
                heads_ref[kv, :, g * HD : (g + 1) * HD],
                projected[block * HD : (block + 1) * HD],
                preferred_element_type=jnp.float32,
            )
            weight = jnp.dot(
                picked_ref[kv * group + g], which, preferred_element_type=jnp.float32
            )
            total = total + match * weight
    out_ref[...] = total.astype(jnp.bfloat16)


def owner_scores(kv_of_block, rows, values, heads, picked, tokens_of_slot):
    slots, width = rows.shape
    targets = heads.shape[1]
    block = 512
    return pl.pallas_call(
        functools.partial(score_kernel, kv_of_block),
        grid=(slots // block,),
        in_specs=[
            pl.BlockSpec((block, width), lambda i: (i, 0)),
            pl.BlockSpec(values.shape, lambda i: (0, 0)),
            pl.BlockSpec(heads.shape, lambda i: (0, 0, 0)),
            pl.BlockSpec(picked.shape, lambda i: (0, 0, 0)),
            pl.BlockSpec((1, block), lambda i: (0, i)),
        ],
        out_specs=pl.BlockSpec((targets, block), lambda i: (0, i)),
        out_shape=jax.ShapeDtypeStruct((targets, slots), jnp.bfloat16),
        compiler_params=pltpu.CompilerParams(vmem_limit_bytes=48 * 1024 * 1024),
    )(rows, values, heads, picked, tokens_of_slot)


def place_kernel(replies_ref, place_ref, scale_ref, out_ref):
    capacity = replies_ref.shape[2]
    slots = place_ref.shape[1]
    total = jnp.zeros(out_ref.shape, jnp.float32)
    spots = lax.broadcasted_iota(jnp.int32, (capacity, slots), 0)
    for owner in range(replies_ref.shape[0]):
        which = jnp.where(spots + owner * capacity == place_ref[...], 1.0, 0.0)
        total = total + jnp.dot(
            replies_ref[owner], which.astype(jnp.bfloat16), preferred_element_type=jnp.float32
        )
    out_ref[...] = (total * scale_ref[...]).astype(jnp.bfloat16)


def on_device(
    decoder,
    value_weight,
    out_weight,
    target_enc,
    target_pos,
    attention,
    norm_gain,
    norm_rstd,
    source_owner,
    source_row,
    source_act,
    source_valid,
):
    n_feat = lax.axis_size("feat")
    n_tgt = lax.axis_size("tgt")
    me_tgt = lax.axis_index("tgt")
    shard = decoder[0]
    shard_rows = shard.shape[0]
    slot_count = source_row.shape[0]
    capacity = max(2, 2 * slot_count // n_feat)
    gains = norm_gain[0]
    positions = target_pos[0]
    targets = positions.shape[0]
    owners = source_owner[:, 0]

    def shifted(x, step):
        return lax.ppermute(x, "tgt", [(i, (i + step) % n_tgt) for i in range(n_tgt)])

    gained_values = (value_weight[0].astype(jnp.float32) * gains[2]).astype(jnp.bfloat16)
    n_grp = lax.axis_size("grp")
    me_grp = lax.axis_index("grp")
    kv_of_block = list(range(KV))
    whole_heads = gained_values.shape[0] == n_grp * HD and n_grp == 2
    if whole_heads:
        half = lax.dynamic_slice_in_dim(gained_values, me_grp * HD, HD)
        target_enc, half = lax.optimization_barrier((target_enc, half))
        kv_of_block = [n_grp * j + g for g in range(n_grp) for j in range(n_feat)]
        values = lax.all_gather(half, ("grp", "feat"), axis=0, tiled=True)
    else:
        values = lax.all_gather(gained_values, "feat", axis=0, tiled=True)

    member = (owners[:, None] == jnp.arange(n_feat, dtype=jnp.int32)[None, :]).astype(jnp.int32)
    ranks = jnp.sum((jnp.cumsum(member, axis=0) - 1) * member, axis=1)
    flat_slot = owners * capacity + ranks
    token_here = jnp.arange(slot_count, dtype=jnp.int32) // K
    asked = jnp.sum(
        jnp.where(
            flat_slot[None, :] == jnp.arange(n_feat * capacity, dtype=jnp.int32)[:, None],
            (token_here * shard_rows + source_row + 1)[None, :],
            0,
        ),
        axis=1,
    )
    asked = lax.all_to_all(
        asked.reshape(n_feat, capacity), "feat", split_axis=0, concat_axis=0, tiled=True
    )
    spare = jnp.arange(n_feat * capacity, dtype=jnp.int32).reshape(n_feat, capacity)
    asked = jnp.where(asked > 0, asked - 1, spare * 8 % shard_rows)
    rows = gather_rows(shard, (asked % shard_rows).reshape(-1))
    tok_dev = attention.shape[2]
    tokens_of_slot = asked // shard_rows + (
        jnp.arange(n_feat, dtype=jnp.int32) * tok_dev
    )[:, None]

    rstd_table = norm_rstd[0]
    tokens_all = rstd_table.shape[1]
    pos_table = (positions[:, None] == jnp.arange(tokens_all, dtype=jnp.int32)[None, :]).astype(
        jnp.float32
    )
    target_scale = jnp.dot(
        pos_table, rstd_table[0] * rstd_table[1], precision=lax.Precision.HIGHEST
    )
    enc_scaled = (target_enc[0].astype(jnp.float32) * gains[0] * gains[1]).astype(jnp.bfloat16)
    partial_heads = jnp.dot(enc_scaled, out_weight[0].T, preferred_element_type=jnp.float32)
    own_targets = targets // n_tgt

    def part(x, of):
        return lax.dynamic_slice_in_dim(x, of * own_targets, own_targets)

    summed_heads = part(partial_heads, me_tgt)
    for step in range(1, n_tgt):
        summed_heads = summed_heads + shifted(part(partial_heads, (me_tgt + step) % n_tgt), step)
    heads_local = (summed_heads * part(target_scale, me_tgt)[:, None]).astype(jnp.bfloat16)
    attn_local = attention[0].astype(jnp.bfloat16)
    pair = HEADS // KV * HD
    if whole_heads:
        own_kv = heads_local.shape[1] // pair
        attn_part = lax.dynamic_slice_in_dim(
            attn_local.reshape(n_tgt, -1, pair), me_tgt, 1
        )[0]
        sent = jnp.concatenate(
            [
                heads_local.reshape(own_targets, own_kv, pair).transpose(1, 0, 2).reshape(-1, pair),
                attn_part,
            ],
            axis=0,
        )
        got = lax.all_to_all(
            jnp.broadcast_to(sent[None], (n_tgt * n_feat,) + sent.shape),
            ("tgt", "feat"),
            split_axis=0,
            concat_axis=0,
            tiled=True,
        )
        cut = own_kv * own_targets
        heads_back = got[:, :cut].reshape(n_tgt, n_feat, own_kv, own_targets, pair)
        heads_back = heads_back.transpose(1, 2, 0, 3, 4).reshape(KV, targets, pair)
        attn_all = got[:, cut:].reshape(n_tgt, n_feat, -1).transpose(1, 0, 2)
        attn_all = attn_all.reshape((n_feat,) + attn_local.shape)
        attn_all = attn_all.transpose(1, 0, 2, 3).reshape(HEADS, tokens_all, tokens_all)
    else:
        heads_back = lax.all_gather(heads_local, "feat", axis=1, tiled=True)
        heads_back = lax.all_gather(heads_back, "tgt", axis=0, tiled=True)
        heads_back = heads_back.reshape(targets, KV, pair).transpose(1, 0, 2)
        attn_all = lax.all_gather(attn_local, "feat", axis=1, tiled=True)
    chosen = jnp.einsum(
        "fq,htq->hft",
        pos_table.astype(jnp.bfloat16),
        attn_all,
        preferred_element_type=jnp.float32,
    )
    causal = jnp.arange(tokens_all, dtype=jnp.int32)[None, :] <= positions[:, None]
    picked = jnp.where(causal[None], chosen, 0.0).astype(jnp.bfloat16)

    raw = owner_scores(kv_of_block, rows, values, heads_back, picked, tokens_of_slot.reshape(1, -1))
    scores = part(raw, me_tgt).astype(jnp.float32)
    for step in range(1, n_tgt):
        scores = scores + shifted(part(raw, (me_tgt + step) % n_tgt), step).astype(jnp.float32)
    replies = lax.all_to_all(
        scores.astype(jnp.bfloat16).reshape(own_targets, n_feat, capacity).transpose(1, 0, 2),
        "feat",
        split_axis=0,
        concat_axis=0,
        tiled=True,
    )
    local_rstd = lax.dynamic_slice_in_dim(
        rstd_table[2], lax.axis_index("feat") * tok_dev, tok_dev
    )
    source_scale = jnp.repeat(local_rstd, K) * source_act * source_valid.astype(jnp.float32)
    return pl.pallas_call(
        place_kernel,
        out_shape=jax.ShapeDtypeStruct((own_targets, slot_count), jnp.bfloat16),
        compiler_params=pltpu.CompilerParams(vmem_limit_bytes=32 * 1024 * 1024),
    )(replies, flat_slot[None, :], source_scale[None, :])[None]


def solution(mesh):
    in_specs = (
        P("lay", "feat", "tgt"),
        P("lay", "feat", "tgt"),
        P("lay", "feat", "tgt"),
        P("lay", "grp", "tgt"),
        P("lay", "grp"),
        P("lay", "grp", "feat", None),
        P("lay", None, "tgt"),
        P("lay", "grp", None),
        P(("grp", "feat"), None),
        P(("grp", "feat")),
        P(("grp", "feat")),
        P(("grp", "feat")),
    )
    out_specs = P("lay", ("grp", "tgt"), "feat")
    return jax.shard_map(
        on_device, mesh=mesh, in_specs=in_specs, out_specs=out_specs, check_vma=False
    )
```

```python
import functools
import jax
import jax.numpy as jnp
from jax import lax
from jax.experimental import pallas as pl
from jax.experimental.pallas import tpu as pltpu
from jax.sharding import PartitionSpec as P

HEADS = 16
KV = 8
HD = 128
K = 128


def gather_kernel(index_ref, shard_ref, out_ref, held, sems):
    step = pl.program_id(0)
    steps = pl.num_programs(0)
    block = out_ref.shape[0]
    width = out_ref.shape[1]

    def fetch(of, slot):
        @pl.loop(0, block, unroll=8)
        def _(i):
            pltpu.make_async_copy(
                shard_ref.at[index_ref[of * block + i] // 8], held.at[slot, i], sems.at[slot]
            ).start()

    @pl.when(step == 0)
    def _():
        fetch(0, 0)

    @pl.when(step + 1 < steps)
    def _():
        fetch(step + 1, (step + 1) % 2)

    now = step % 2
    pltpu.make_async_copy(shard_ref.at[pl.ds(0, block)], held.at[now], sems.at[now]).wait()
    sublane = lax.broadcasted_iota(jnp.int32, (8, width), 0)

    @pl.loop(0, block // 16)
    def _(chunk):
        halves = []
        for half in range(2):
            kept = jnp.zeros((8, width), jnp.float32)
            for u in range(8):
                i = chunk * 16 + half * 8 + u
                row = index_ref[step * block + i] % 8
                group = held[now, i].astype(jnp.float32)
                turned = pltpu.roll(group, (u + 8 - row) % 8, 0)
                kept = jnp.where(sublane == u, turned, kept)
            halves.append(kept)
        out_ref[pl.ds(pl.multiple_of(chunk * 16, 16), 16), :] = jnp.concatenate(
            halves, axis=0
        ).astype(jnp.bfloat16)


def gather_rows(shard, index):
    slots = index.shape[0]
    width = shard.shape[1]
    block = 64
    return pl.pallas_call(
        gather_kernel,
        grid_spec=pltpu.PrefetchScalarGridSpec(
            num_scalar_prefetch=1,
            grid=(slots // block,),
            in_specs=[pl.BlockSpec(memory_space=pl.ANY)],
            out_specs=pl.BlockSpec((block, width), lambda i, index: (i, 0)),
            scratch_shapes=[
                pltpu.VMEM((2, block, 8, width), jnp.bfloat16),
                pltpu.SemaphoreType.DMA((2,)),
            ],
        ),
        out_shape=jax.ShapeDtypeStruct((slots, width), jnp.bfloat16),
        compiler_params=pltpu.CompilerParams(vmem_limit_bytes=24 * 1024 * 1024),
        cost_estimate=pl.CostEstimate(
            flops=slots * width * 16, bytes_accessed=slots * width * 18, transcendentals=0
        ),
    )(index, shard.reshape(shard.shape[0] // 8, 8, width))


def score_kernel(kv_of_block, rows_ref, values_ref, heads_ref, picked_ref, token_ref, *more):
    out_ref = more[-1]
    group = HEADS // KV
    projected = lax.dot_general(
        values_ref[...],
        rows_ref[...],
        (((1,), (1,)), ((), ())),
        preferred_element_type=jnp.float32,
    ).astype(jnp.bfloat16)
    tokens = picked_ref.shape[2]
    slots = token_ref.shape[1]
    which = lax.broadcasted_iota(jnp.int32, (tokens, slots), 0) == token_ref[...]
    which = jnp.where(which, 1.0, 0.0).astype(jnp.bfloat16)
    total = more[0][...] if len(more) == 2 else jnp.zeros(out_ref.shape, jnp.float32)
    for block in range(len(kv_of_block)):
        kv = kv_of_block[block]
        for g in range(group):
            match = jnp.dot(
                heads_ref[kv, :, g * HD : (g + 1) * HD],
                projected[block * HD : (block + 1) * HD],
                preferred_element_type=jnp.float32,
            )
            weight = jnp.dot(
                picked_ref[kv * group + g], which, preferred_element_type=jnp.float32
            )
            total = total + match * weight
    out_ref[...] = total.astype(out_ref.dtype)


def owner_scores(kv_of_block, rows, values, heads, picked, tokens_of_slot, dtype, base=()):
    slots, width = rows.shape
    targets = heads.shape[1]
    block = 512
    return pl.pallas_call(
        functools.partial(score_kernel, kv_of_block),
        grid=(slots // block,),
        in_specs=[
            pl.BlockSpec((block, width), lambda i: (i, 0)),
            pl.BlockSpec(values.shape, lambda i: (0, 0)),
            pl.BlockSpec(heads.shape, lambda i: (0, 0, 0)),
            pl.BlockSpec(picked.shape, lambda i: (0, 0, 0)),
            pl.BlockSpec((1, block), lambda i: (0, i)),
        ]
        + [pl.BlockSpec((targets, block), lambda i: (0, i))] * len(base),
        out_specs=pl.BlockSpec((targets, block), lambda i: (0, i)),
        out_shape=jax.ShapeDtypeStruct((targets, slots), dtype),
        compiler_params=pltpu.CompilerParams(vmem_limit_bytes=48 * 1024 * 1024),
        cost_estimate=pl.CostEstimate(
            flops=2 * slots * values.shape[0] * (width + 4 * targets),
            bytes_accessed=2 * slots * width,
            transcendentals=0,
        ),
    )(rows, values, heads, picked, tokens_of_slot, *base)


def place_kernel(replies_ref, place_ref, scale_ref, out_ref):
    capacity = replies_ref.shape[2]
    slots = place_ref.shape[1]
    total = jnp.zeros(out_ref.shape, jnp.float32)
    spots = lax.broadcasted_iota(jnp.int32, (capacity, slots), 0)
    for owner in range(replies_ref.shape[0]):
        which = jnp.where(spots + owner * capacity == place_ref[...], 1.0, 0.0)
        total = total + jnp.dot(
            replies_ref[owner], which.astype(jnp.bfloat16), preferred_element_type=jnp.float32
        )
    out_ref[...] = (total * scale_ref[...]).astype(jnp.bfloat16)


def on_device(
    decoder,
    value_weight,
    out_weight,
    target_enc,
    target_pos,
    attention,
    norm_gain,
    norm_rstd,
    source_owner,
    source_row,
    source_act,
    source_valid,
):
    n_feat = lax.axis_size("feat")
    n_tgt = lax.axis_size("tgt")
    me_tgt = lax.axis_index("tgt")
    shard = decoder[0]
    shard_rows = shard.shape[0]
    slot_count = source_row.shape[0]
    capacity = max(2, 2 * slot_count // n_feat)
    gains = norm_gain[0]
    positions = target_pos[0]
    targets = positions.shape[0]
    owners = source_owner[:, 0]

    def shifted(x, step):
        return lax.ppermute(x, "tgt", [(i, (i + step) % n_tgt) for i in range(n_tgt)])

    gained_values = (value_weight[0].astype(jnp.float32) * gains[2]).astype(jnp.bfloat16)
    n_grp = lax.axis_size("grp")
    kv_of_block = [list(range(KV))]
    whole_heads = gained_values.shape[0] == n_grp * HD and n_grp == 2
    if whole_heads:
        values = [
            lax.all_gather(gained_values[g * HD : (g + 1) * HD], "feat", axis=0, tiled=True)
            for g in range(2)
        ]
        kv_of_block = [[2 * j + g for j in range(n_feat)] for g in range(2)]
    else:
        values = [lax.all_gather(gained_values, "feat", axis=0, tiled=True)]

    member = (owners[:, None] == jnp.arange(n_feat, dtype=jnp.int32)[None, :]).astype(jnp.int32)
    ranks = jnp.sum((jnp.cumsum(member, axis=0) - 1) * member, axis=1)
    flat_slot = owners * capacity + ranks
    token_here = jnp.arange(slot_count, dtype=jnp.int32) // K
    asked = jnp.sum(
        jnp.where(
            flat_slot[None, :] == jnp.arange(n_feat * capacity, dtype=jnp.int32)[:, None],
            (token_here * shard_rows + source_row + 1)[None, :],
            0,
        ),
        axis=1,
    )
    asked = lax.all_to_all(
        asked.reshape(n_feat, capacity), "feat", split_axis=0, concat_axis=0, tiled=True
    )
    spare = jnp.arange(n_feat * capacity, dtype=jnp.int32).reshape(n_feat, capacity)
    asked = jnp.where(asked > 0, asked - 1, spare * 8 % shard_rows)
    rows = gather_rows(shard, (asked % shard_rows).reshape(-1))
    tok_dev = attention.shape[2]
    tokens_of_slot = asked // shard_rows + (
        jnp.arange(n_feat, dtype=jnp.int32) * tok_dev
    )[:, None]

    rstd_table = norm_rstd[0]
    tokens_all = rstd_table.shape[1]
    pos_table = (positions[:, None] == jnp.arange(tokens_all, dtype=jnp.int32)[None, :]).astype(
        jnp.float32
    )
    target_scale = jnp.dot(
        pos_table, rstd_table[0] * rstd_table[1], precision=lax.Precision.HIGHEST
    )
    enc_scaled = (target_enc[0].astype(jnp.float32) * gains[0] * gains[1]).astype(jnp.bfloat16)
    partial_heads = jnp.dot(enc_scaled, out_weight[0].T, preferred_element_type=jnp.float32)
    own_targets = targets // n_tgt

    def part(x, of):
        return lax.dynamic_slice_in_dim(x, of * own_targets, own_targets)

    summed_heads = part(partial_heads, me_tgt)
    for step in range(1, n_tgt):
        summed_heads = summed_heads + shifted(part(partial_heads, (me_tgt + step) % n_tgt), step)
    heads_local = (summed_heads * part(target_scale, me_tgt)[:, None]).astype(jnp.bfloat16)
    attn_local = attention[0].astype(jnp.bfloat16)
    pair = HEADS // KV * HD
    if whole_heads:
        own_kv = heads_local.shape[1] // pair
        attn_part = lax.dynamic_slice_in_dim(
            attn_local.reshape(n_tgt, -1, pair), me_tgt, 1
        )[0]
        sent = jnp.concatenate(
            [
                heads_local.reshape(own_targets, own_kv, pair).transpose(1, 0, 2).reshape(-1, pair),
                attn_part,
            ],
            axis=0,
        )
        got = lax.all_to_all(
            jnp.broadcast_to(sent[None], (n_tgt * n_feat,) + sent.shape),
            ("tgt", "feat"),
            split_axis=0,
            concat_axis=0,
            tiled=True,
        )
        cut = own_kv * own_targets
        heads_back = got[:, :cut].reshape(n_tgt, n_feat, own_kv, own_targets, pair)
        heads_back = heads_back.transpose(1, 2, 0, 3, 4).reshape(KV, targets, pair)
        attn_all = got[:, cut:].reshape(n_tgt, n_feat, -1).transpose(1, 0, 2)
        attn_all = attn_all.reshape((n_feat,) + attn_local.shape)
        attn_all = attn_all.transpose(1, 0, 2, 3).reshape(HEADS, tokens_all, tokens_all)
    else:
        heads_back = lax.all_gather(heads_local, "feat", axis=1, tiled=True)
        heads_back = lax.all_gather(heads_back, "tgt", axis=0, tiled=True)
        heads_back = heads_back.reshape(targets, KV, pair).transpose(1, 0, 2)
        attn_all = lax.all_gather(attn_local, "feat", axis=1, tiled=True)
    chosen = jnp.einsum(
        "fq,htq->hft",
        pos_table.astype(jnp.bfloat16),
        attn_all,
        preferred_element_type=jnp.float32,
    )
    causal = jnp.arange(tokens_all, dtype=jnp.int32)[None, :] <= positions[:, None]
    picked = jnp.where(causal[None], chosen, 0.0).astype(jnp.bfloat16)

    base = ()
    for i in range(len(values)):
        dtype = jnp.bfloat16 if i == len(values) - 1 else jnp.float32
        raw = owner_scores(
            kv_of_block[i],
            rows,
            values[i],
            heads_back,
            picked,
            tokens_of_slot.reshape(1, -1),
            dtype,
            base,
        )
        base = (raw,)
    scores = part(raw, me_tgt).astype(jnp.float32)
    for step in range(1, n_tgt):
        scores = scores + shifted(part(raw, (me_tgt + step) % n_tgt), step).astype(jnp.float32)
    replies = lax.all_to_all(
        scores.astype(jnp.bfloat16).reshape(own_targets, n_feat, capacity).transpose(1, 0, 2),
        "feat",
        split_axis=0,
        concat_axis=0,
        tiled=True,
    )
    local_rstd = lax.dynamic_slice_in_dim(
        rstd_table[2], lax.axis_index("feat") * tok_dev, tok_dev
    )
    source_scale = jnp.repeat(local_rstd, K) * source_act * source_valid.astype(jnp.float32)
    return pl.pallas_call(
        place_kernel,
        out_shape=jax.ShapeDtypeStruct((own_targets, slot_count), jnp.bfloat16),
        compiler_params=pltpu.CompilerParams(vmem_limit_bytes=32 * 1024 * 1024),
    )(replies, flat_slot[None, :], source_scale[None, :])[None]


def solution(mesh):
    in_specs = (
        P("lay", "feat", "tgt"),
        P("lay", "feat", "tgt"),
        P("lay", "feat", "tgt"),
        P("lay", "grp", "tgt"),
        P("lay", "grp"),
        P("lay", "grp", "feat", None),
        P("lay", None, "tgt"),
        P("lay", "grp", None),
        P(("grp", "feat"), None),
        P(("grp", "feat")),
        P(("grp", "feat")),
        P(("grp", "feat")),
    )
    out_specs = P("lay", ("grp", "tgt"), "feat")
    return jax.shard_map(
        on_device, mesh=mesh, in_specs=in_specs, out_specs=out_specs, check_vma=False
    )
```
